32 devices in a mesh: group: 2 (over y), weight: 4 (over z), dp: 4 (over x, core).
Axes of the slice: x: 2, y: 2, z: 4, core: 2. Of those that a mesh axis runs over, the one named last changes fastest.
Arguments:
- tapped: bfloat16 [3, 4096, 4096], P(None, ('group', 'dp'), 'weight'), parts along dimension 1, may hold values from -6 to 6
- join_weight: bfloat16 [3, 4096, 4096], P(None, 'weight', 'dp')
- norm_gain: float32 [4096], P('weight'), may hold values from 0.1 to 1.9
- cotangent: bfloat16 [4096, 4096], P(('group', 'dp'), 'weight'), parts along dimension 0, may hold values from -0.13183594 to 0.13183594
- live_mask: int32 [4096], P(('group', 'dp')), parts along dimension 0, may hold values 0 or 1
Outputs:
- hidden: bfloat16 [4096, 4096], P(('group', 'dp'), 'weight'), parts along dimension 0
- grad_weight: bfloat16 [6, 4096, 4096], P('group', 'weight'), parts along dimension 0
- grad_gain: float32 [8192], P(('group', 'weight')), parts along dimension 0
The draws below stay inside these ranges and needn't reach their ends.
There are 2 independent parts, one for each index of `group`. The reference program is written for one: setup_inputs(seed, part) draws one part's arguments, and reference() takes and returns one part's arrays. A program takes and returns all parts, laid end to end along the dimension named above; an argument that names none is the same for every part. Nothing has to cross between parts.
All inputs are finite; a program needn't handle non-finite values. No bound on the sum of `live_mask` on one device may be relied on, other than what follows from the above.
Results may differ from the reference program's by a relative error of at most 0.014.
Values may be sent and summed in bfloat16 or wider, within the bound.
A program may use at most 128 MiB of HBM per device.

```python
import jax
import jax.numpy as jnp
from jax import lax

D = 4096
LEVELS = 3
TOK_DEV = 512
TOKENS = 2048
N_WEIGHT = 4
N_DP = 4


def draw_join_weight(key, part):
    key = jax.random.fold_in(key, 11)
    column = jnp.arange(D, dtype=jnp.float32) / D
    base = jax.random.normal(key, (LEVELS, D, D), jnp.float32)
    rising = 3.0 ** column
    return (base * rising[None, None, :] / jnp.sqrt(3.0 * D)).astype(jnp.bfloat16)


def plant(result, own_key, low, high):
    spot = [jax.random.randint(jax.random.fold_in(own_key, axis), (), 0, length) for axis, length in enumerate(result.shape)]
    widest = result.shape.index(max(result.shape))
    next_to = spot[:widest] + [(spot[widest] + 1) % result.shape[widest]] + spot[widest + 1:]
    return result.at[tuple(spot)].set(low).at[tuple(next_to)].set(high)


def levels(stream_key, shape, split, smallest, top_value):
    def one(dim, blocks):
        draws = jax.random.uniform(jax.random.fold_in(jax.random.fold_in(stream_key, 6), dim), (blocks,), jnp.float32, smallest / len(split), top_value / len(split))
        return jnp.repeat(jnp.exp(draws), shape[dim] // blocks).reshape((-1,) + (1,) * (len(shape) - dim - 1))

    gain = one(*split[0])
    for cut in split[1:]:
        gain = gain * one(*cut)
    return gain


def normal_values(own_key, dims, spread, limit, cuts=(), kind=jnp.bfloat16):
    array = spread * jax.random.normal(own_key, dims, jnp.float32)
    if cuts:
        array = array * levels(own_key, dims, cuts, -0.22, 0.18)
    return jnp.clip(array, -limit, limit).astype(kind)


def setup_inputs(seed: int = 0, part: int = 0) -> dict:
    splits = jax.random.split(jax.random.key(seed), 6)
    own_keys = jax.random.split(jax.random.fold_in(splits[5], part), 6)
    tapped = normal_values(own_keys[0], (LEVELS, TOKENS, D), 1.0, 6.0, ((1, 4), (2, 4)))
    join_weight = draw_join_weight(jax.random.fold_in(splits[5], 71), part)
    norm_gain = jnp.clip(1.0 + 0.18 * jax.random.normal(splits[2], (D,), jnp.float32), 0.1, 1.9)
    cotangent = normal_values(own_keys[3], (TOKENS, D), ((TOK_DEV * N_DP) ** -0.5), 0.13183594, ((0, 4), (1, 4)))
    live_mask = plant((jax.random.randint(own_keys[4], (TOKENS,), 0, 8) < 7).astype(jnp.int32), jax.random.fold_in(own_keys[4], 1), 0, 1)
    return {"tapped": tapped, "join_weight": join_weight, "norm_gain": norm_gain, "cotangent": cotangent, "live_mask": live_mask}


epsilon = 1e-06

def reference(tapped, join_weight, norm_gain, cotangent, live_mask):
    local_rows = D // N_WEIGHT
    tapped_split = tapped.reshape(LEVELS, TOKENS, N_WEIGHT, local_rows).transpose(2, 0, 1, 3)
    weight_split = join_weight.reshape(LEVELS, N_WEIGHT, local_rows, D).transpose(1, 0, 2, 3)

    def forward_step(total, pieces):
        inputs, weights = pieces
        term = jnp.einsum('ktr,krc->tc', inputs.astype(jnp.float32), weights.astype(jnp.float32))
        rounded = lax.optimization_barrier(term.astype(jnp.bfloat16))
        return (total + rounded.astype(jnp.float32), None)
    combined, unused = lax.scan(forward_step, jnp.zeros((TOKENS, D), jnp.float32), (tapped_split, weight_split))
    squares = lax.optimization_barrier(jnp.mean(combined * combined, axis=1))
    inverse = lax.rsqrt(squares + epsilon)
    hidden = (combined * inverse[:, None] * norm_gain[None, :]).astype(jnp.bfloat16)
    wanted = cotangent.astype(jnp.float32) * live_mask[:, None].astype(jnp.float32)
    scaled = wanted * norm_gain[None, :]
    projected = lax.optimization_barrier(jnp.mean(scaled * combined, axis=1))
    joined_grad = (inverse[:, None] * (scaled - combined * (inverse * inverse * projected)[:, None])).astype(jnp.bfloat16)
    gain_terms = wanted * combined * inverse[:, None]
    tapped_blocks = tapped.reshape(LEVELS, N_DP, TOK_DEV, D).transpose(1, 0, 2, 3)
    grad_blocks = joined_grad.reshape(N_DP, TOK_DEV, D)
    gain_blocks = gain_terms.reshape(N_DP, TOK_DEV, D)

    def backward_step(totals, pieces):
        inputs, errors, gains = pieces
        term = jnp.einsum('ktr,tc->krc', inputs.astype(jnp.float32), errors.astype(jnp.float32))
        gain_part = lax.optimization_barrier(jnp.sum(gains, axis=0))
        rounded = lax.optimization_barrier((term.astype(jnp.bfloat16), gain_part.astype(jnp.bfloat16)))
        return ((totals[0] + rounded[0].astype(jnp.float32), totals[1] + rounded[1].astype(jnp.float32)), None)
    start_totals = (jnp.zeros((LEVELS, D, D), jnp.float32), jnp.zeros((D,), jnp.float32))
    totals, unused_back = lax.scan(backward_step, start_totals, (tapped_blocks, grad_blocks, gain_blocks))
    return (hidden, totals[0].astype(jnp.bfloat16), totals[1])
```

```python
import functools

import jax
import jax.numpy as jnp
from jax import lax
from jax.sharding import PartitionSpec as P

epsilon = 1e-06
TOKEN_PARTS = 2
COLUMN_PARTS = 2


def on_device(tapped, join_weight, norm_gain, cotangent, live_mask):
    full_rows = lax.all_gather(join_weight, "dp", axis=2, tiled=True)
    feature_count = full_rows.shape[2]
    combined = lax.psum_scatter(
        jnp.einsum("krc,ktr->ct", full_rows, tapped, preferred_element_type=jnp.float32).astype(
            jnp.bfloat16
        ),
        "weight",
        scatter_dimension=0,
        tiled=True,
    ).astype(jnp.float32)
    gain_column = norm_gain[:, None]
    wanted = cotangent.T.astype(jnp.float32) * live_mask[None, :].astype(jnp.float32)
    scaled = wanted * gain_column
    square_total = lax.psum(jnp.sum(combined * combined, axis=0), "weight")
    cross_total = lax.psum(jnp.sum(scaled * combined, axis=0), "weight")
    inverse = lax.rsqrt(square_total / feature_count + epsilon)
    projected = cross_total / feature_count
    hidden = (combined * inverse[None, :] * gain_column).T.astype(jnp.bfloat16)
    joined_grad = (
        inverse[None, :] * (scaled - combined * (inverse * inverse * projected)[None, :])
    ).astype(jnp.bfloat16)
    grad_term = jnp.einsum(
        "ktr,ct->krc",
        tapped,
        lax.all_gather(joined_grad, "weight", axis=0, tiled=True),
        preferred_element_type=jnp.float32,
    )
    gain_term = jnp.sum(wanted * combined * inverse[None, :], axis=1)
    grad_weight, grad_gain = (
        lax.psum(grad_term.astype(jnp.bfloat16), "dp").astype(jnp.float32),
        lax.psum(gain_term.astype(jnp.bfloat16), "dp").astype(jnp.float32),
    )
    return (hidden, grad_weight.astype(jnp.bfloat16), grad_gain)


def partner(count, flip):
    return [(index, index ^ flip) for index in range(count)]


def transposed(count):
    return [(w * count + d, d * count + w) for w in range(count) for d in range(count)]


def on_square(count, tapped, join_weight, norm_gain, cotangent, live_mask):
    swap = transposed(count)
    levels, tokens, rows = tapped.shape
    columns = join_weight.shape[2]
    feature_count = columns * count

    def turn(block):
        return lax.ppermute(block, ("weight", "dp"), swap)

    wanted = turn(cotangent * live_mask[:, None].astype(cotangent.dtype)).astype(jnp.float32)
    gain_row = turn(norm_gain)[None, :]
    part = tokens // TOKEN_PARTS
    gathered, pieces = [], []
    for s in range(TOKEN_PARTS):
        block = lax.all_gather(tapped[:, s * part : (s + 1) * part], "dp", axis=0)
        gathered.append(block)
        partial = jnp.einsum(
            "dktr,krc->dtc", block, join_weight, preferred_element_type=jnp.float32
        ).astype(jnp.bfloat16)
        pieces.append(lax.psum_scatter(partial, "weight", scatter_dimension=0, tiled=False))
    all_tapped = jnp.concatenate(gathered, axis=2)
    combined = jnp.concatenate(pieces, axis=0).astype(jnp.float32)
    scaled = wanted * gain_row
    sums = lax.psum(
        jnp.stack([jnp.sum(combined * combined, axis=1), jnp.sum(scaled * combined, axis=1)]), "dp"
    )
    inverse = lax.rsqrt(sums[0] / feature_count + epsilon)[:, None]
    projected = (sums[1] / feature_count)[:, None]
    joined_grad = (
        inverse * (scaled - combined * (inverse * inverse * projected))
    ).astype(jnp.bfloat16)
    hidden = turn((combined * inverse * gain_row).astype(jnp.bfloat16))
    gain_term = jnp.sum(wanted * combined * inverse, axis=0).astype(jnp.bfloat16)
    grad_gain = turn(lax.psum(gain_term.astype(jnp.float32), "weight"))

    me = lax.axis_index("dp")
    width = columns // COLUMN_PARTS
    grad_weight = jnp.zeros((levels, rows, feature_count), jnp.bfloat16)

    def put(total, errors, owner, c):
        term = jnp.einsum(
            "dktr,dtc->krc", all_tapped, errors, preferred_element_type=jnp.float32
        ).astype(jnp.bfloat16)
        return lax.dynamic_update_slice(total, term, (0, 0, owner * columns + c * width))

    mine = [
        lax.all_gather(joined_grad[:, c * width : (c + 1) * width], "weight", axis=0)
        for c in range(COLUMN_PARTS)
    ]
    far = [lax.ppermute(block, "dp", partner(count, 2)) for block in mine]
    near = [lax.ppermute(block, "dp", partner(count, 1)) for block in mine]
    last = [lax.ppermute(block, "dp", partner(count, 1)) for block in far]
    for blocks, flip in ((mine, 0), (near, 1), (far, 2), (last, 3)):
        for c, block in enumerate(blocks):
            grad_weight = put(grad_weight, block, me ^ flip, c)
    return (hidden, grad_weight, grad_gain)


def solution(mesh):
    count = mesh.shape["dp"]
    square = count == 4 and mesh.shape["weight"] == count
    return jax.shard_map(
        functools.partial(on_square, count) if square else on_device,
        mesh=mesh,
        in_specs=(
            P(None, ("group", "dp"), "weight"),
            P(None, "weight", "dp"),
            P("weight"),
            P(("group", "dp"), "weight"),
            P(("group", "dp")),
        ),
        out_specs=(
            P(("group", "dp"), "weight"),
            P("group", "weight", None),
            P(("group", "weight")),
        ),
        check_vma=False,
    )
```

```python
import functools

import jax
import jax.numpy as jnp
from jax import lax
from jax.sharding import PartitionSpec as P

epsilon = 1e-06
TOKEN_PARTS = 2
COLUMN_PARTS = 2


def on_device(tapped, join_weight, norm_gain, cotangent, live_mask):
    full_rows = lax.all_gather(join_weight, "dp", axis=2, tiled=True)
    feature_count = full_rows.shape[2]
    combined = lax.psum_scatter(
        jnp.einsum("krc,ktr->ct", full_rows, tapped, preferred_element_type=jnp.float32).astype(
            jnp.bfloat16
        ),
        "weight",
        scatter_dimension=0,
        tiled=True,
    ).astype(jnp.float32)
    gain_column = norm_gain[:, None]
    wanted = cotangent.T.astype(jnp.float32) * live_mask[None, :].astype(jnp.float32)
    scaled = wanted * gain_column
    square_total = lax.psum(jnp.sum(combined * combined, axis=0), "weight")
    cross_total = lax.psum(jnp.sum(scaled * combined, axis=0), "weight")
    inverse = lax.rsqrt(square_total / feature_count + epsilon)
    projected = cross_total / feature_count
    hidden = (combined * inverse[None, :] * gain_column).T.astype(jnp.bfloat16)
    joined_grad = (
        inverse[None, :] * (scaled - combined * (inverse * inverse * projected)[None, :])
    ).astype(jnp.bfloat16)
    grad_term = jnp.einsum(
        "ktr,ct->krc",
        tapped,
        lax.all_gather(joined_grad, "weight", axis=0, tiled=True),
        preferred_element_type=jnp.float32,
    )
    gain_term = jnp.sum(wanted * combined * inverse[None, :], axis=1)
    grad_weight, grad_gain = (
        lax.psum(grad_term.astype(jnp.bfloat16), "dp").astype(jnp.float32),
        lax.psum(gain_term.astype(jnp.bfloat16), "dp").astype(jnp.float32),
    )
    return (hidden, grad_weight.astype(jnp.bfloat16), grad_gain)


def partner(count, flip):
    return [(index, index ^ flip) for index in range(count)]


def transposed(count):
    return [(w * count + d, d * count + w) for w in range(count) for d in range(count)]


def on_square(count, tapped, join_weight, norm_gain, cotangent, live_mask):
    swap = transposed(count)
    levels, tokens, rows = tapped.shape
    columns = join_weight.shape[2]
    feature_count = columns * count

    def turn(block):
        return lax.ppermute(block, ("weight", "dp"), swap)

    wanted = turn(cotangent * live_mask[:, None].astype(cotangent.dtype))
    gain_row = turn(norm_gain)[None, :]
    part = tokens // TOKEN_PARTS
    gathered, pieces = [], []
    for s in range(TOKEN_PARTS):
        block = lax.all_gather(tapped[:, s * part : (s + 1) * part], "dp", axis=0)
        if s == 0:
            block, wanted, gain_row = lax.optimization_barrier((block, wanted, gain_row))
        gathered.append(block)
        partial = jnp.einsum(
            "dktr,krc->dtc", block, join_weight, preferred_element_type=jnp.float32
        ).astype(jnp.bfloat16)
        pieces.append(lax.psum_scatter(partial, "weight", scatter_dimension=0, tiled=False))
    all_tapped = jnp.concatenate(gathered, axis=2)
    combined = jnp.concatenate(pieces, axis=0).astype(jnp.float32)
    wanted = wanted.astype(jnp.float32)
    scaled = wanted * gain_row
    sums = lax.psum(
        jnp.stack([jnp.sum(combined * combined, axis=1), jnp.sum(scaled * combined, axis=1)]), "dp"
    )
    inverse = lax.rsqrt(sums[0] / feature_count + epsilon)[:, None]
    projected = (sums[1] / feature_count)[:, None]
    joined_grad = (
        inverse * (scaled - combined * (inverse * inverse * projected))
    ).astype(jnp.bfloat16)
    normed = (combined * inverse * gain_row).astype(jnp.bfloat16)
    gain_term = jnp.sum(wanted * combined * inverse, axis=0).astype(jnp.bfloat16)

    me = lax.axis_index("dp")
    width = columns // COLUMN_PARTS
    grad_weight = jnp.zeros((levels, rows, feature_count), jnp.bfloat16)

    def put(total, errors, owner, c):
        term = jnp.einsum(
            "dktr,dtc->krc", all_tapped, errors, preferred_element_type=jnp.float32
        ).astype(jnp.bfloat16)
        return lax.dynamic_update_slice(total, term, (0, 0, owner * columns + c * width))

    mine = [
        lax.all_gather(joined_grad[:, c * width : (c + 1) * width], "weight", axis=0)
        for c in range(COLUMN_PARTS)
    ]
    mine[-1], normed = lax.optimization_barrier((mine[-1], normed))
    far = [lax.ppermute(block, "dp", partner(count, 2)) for block in mine]
    far[0], gain_term = lax.optimization_barrier((far[0], gain_term))
    near = [lax.ppermute(block, "dp", partner(count, 1)) for block in mine]
    last = [lax.ppermute(block, "dp", partner(count, 1)) for block in far]
    hidden = turn(normed)
    grad_gain = turn(lax.psum(gain_term.astype(jnp.float32), "weight"))
    for blocks, flip in ((mine, 0), (near, 1), (far, 2), (last, 3)):
        for c, block in enumerate(blocks):
            grad_weight = put(grad_weight, block, me ^ flip, c)
    return (hidden, grad_weight, grad_gain)


def solution(mesh):
    count = mesh.shape["dp"]
    square = count == 4 and mesh.shape["weight"] == count
    return jax.shard_map(
        functools.partial(on_square, count) if square else on_device,
        mesh=mesh,
        in_specs=(
            P(None, ("group", "dp"), "weight"),
            P(None, "weight", "dp"),
            P("weight"),
            P(("group", "dp"), "weight"),
            P(("group", "dp")),
        ),
        out_specs=(
            P(("group", "dp"), "weight"),
            P("group", "weight", None),
            P(("group", "weight")),
        ),
        check_vma=False,
    )
```

```python
import functools

import jax
import jax.numpy as jnp
from jax import lax
from jax.sharding import PartitionSpec as P

epsilon = 1e-06
TOKEN_PARTS = 2
COLUMN_PARTS = 2


def on_device(tapped, join_weight, norm_gain, cotangent, live_mask):
    full_rows = lax.all_gather(join_weight, "dp", axis=2, tiled=True)
    feature_count = full_rows.shape[2]
    combined = lax.psum_scatter(
        jnp.einsum("krc,ktr->ct", full_rows, tapped, preferred_element_type=jnp.float32).astype(
            jnp.bfloat16
        ),
        "weight",
        scatter_dimension=0,
        tiled=True,
    ).astype(jnp.float32)
    gain_column = norm_gain[:, None]
    wanted = cotangent.T.astype(jnp.float32) * live_mask[None, :].astype(jnp.float32)
    scaled = wanted * gain_column
    square_total = lax.psum(jnp.sum(combined * combined, axis=0), "weight")
    cross_total = lax.psum(jnp.sum(scaled * combined, axis=0), "weight")
    inverse = lax.rsqrt(square_total / feature_count + epsilon)
    projected = cross_total / feature_count
    hidden = (combined * inverse[None, :] * gain_column).T.astype(jnp.bfloat16)
    joined_grad = (
        inverse[None, :] * (scaled - combined * (inverse * inverse * projected)[None, :])
    ).astype(jnp.bfloat16)
    grad_term = jnp.einsum(
        "ktr,ct->krc",
        tapped,
        lax.all_gather(joined_grad, "weight", axis=0, tiled=True),
        preferred_element_type=jnp.float32,
    )
    gain_term = jnp.sum(wanted * combined * inverse[None, :], axis=1)
    grad_weight, grad_gain = (
        lax.psum(grad_term.astype(jnp.bfloat16), "dp").astype(jnp.float32),
        lax.psum(gain_term.astype(jnp.bfloat16), "dp").astype(jnp.float32),
    )
    return (hidden, grad_weight.astype(jnp.bfloat16), grad_gain)


def partner(count, flip):
    return [(index, index ^ flip) for index in range(count)]


def transposed(count):
    return [(w * count + d, d * count + w) for w in range(count) for d in range(count)]


def on_square(count, tapped, join_weight, norm_gain, cotangent, live_mask):
    swap = transposed(count)
    levels, tokens, rows = tapped.shape
    columns = join_weight.shape[2]
    feature_count = columns * count

    def turn(block):
        return lax.ppermute(block, ("weight", "dp"), swap)

    wanted = turn(cotangent * live_mask[:, None].astype(cotangent.dtype))
    gain_row = turn(norm_gain)[None, :]
    part = tokens // TOKEN_PARTS
    gathered, pieces = [], []
    for s in range(TOKEN_PARTS):
        block = lax.all_gather(tapped[:, s * part : (s + 1) * part], "dp", axis=0)
        if s == 0:
            block, wanted, gain_row = lax.optimization_barrier((block, wanted, gain_row))
        gathered.append(block)
        partial = jnp.einsum(
            "dktr,krc->dtc", block, join_weight, preferred_element_type=jnp.float32
        ).astype(jnp.bfloat16)
        pieces.append(lax.psum_scatter(partial, "weight", scatter_dimension=0, tiled=False))
    all_tapped = jnp.concatenate(gathered, axis=2)
    combined = jnp.concatenate(pieces, axis=0).astype(jnp.float32)
    wanted = wanted.astype(jnp.float32)
    scaled = wanted * gain_row
    sums = lax.psum(
        jnp.stack([jnp.sum(combined * combined, axis=1), jnp.sum(scaled * combined, axis=1)]), "dp"
    )
    inverse = lax.rsqrt(sums[0] / feature_count + epsilon)[:, None]
    projected = (sums[1] / feature_count)[:, None]
    joined_grad = (
        inverse * (scaled - combined * (inverse * inverse * projected))
    ).astype(jnp.bfloat16)
    normed = (combined * inverse * gain_row).astype(jnp.bfloat16)
    gain_term = jnp.sum(wanted * combined * inverse, axis=0).astype(jnp.bfloat16)

    me = lax.axis_index("dp")
    width = columns // COLUMN_PARTS
    grad_weight = jnp.zeros((levels, rows, feature_count), jnp.bfloat16)

    def put(total, errors, owner, c):
        term = jnp.einsum(
            "dktr,dtc->krc", all_tapped, errors, preferred_element_type=jnp.float32
        ).astype(jnp.bfloat16)
        return lax.dynamic_update_slice(total, term, (0, 0, owner * columns + c * width))

    mine = [
        lax.all_gather(joined_grad[:, c * width : (c + 1) * width], "weight", axis=0)
        for c in range(COLUMN_PARTS)
    ]
    mine[-1], gain_term = lax.optimization_barrier((mine[-1], gain_term))
    far = [lax.ppermute(block, "dp", partner(count, 2)) for block in mine]
    far[0], normed = lax.optimization_barrier((far[0], normed))
    near = [lax.ppermute(block, "dp", partner(count, 1)) for block in mine]
    last = [lax.ppermute(block, "dp", partner(count, 1)) for block in far]
    hidden = turn(normed)
    grad_gain = turn(lax.psum(gain_term.astype(jnp.float32), "weight"))
    for blocks, flip in ((mine, 0), (near, 1), (far, 2), (last, 3)):
        for c, block in enumerate(blocks):
            grad_weight = put(grad_weight, block, me ^ flip, c)
    return (hidden, grad_weight, grad_gain)


def solution(mesh):
    count = mesh.shape["dp"]
    square = count == 4 and mesh.shape["weight"] == count
    return jax.shard_map(
        functools.partial(on_square, count) if square else on_device,
        mesh=mesh,
        in_specs=(
            P(None, ("group", "dp"), "weight"),
            P(None, "weight", "dp"),
            P("weight"),
            P(("group", "dp"), "weight"),
            P(("group", "dp")),
        ),
        out_specs=(
            P(("group", "dp"), "weight"),
            P("group", "weight", None),
            P(("group", "weight")),
        ),
        check_vma=False,
    )
```
